1024 devices in a mesh: rep: 32 (over x_lo, z), fsdp: 32 (over x_hi, y, core).
Axes of the slice: x: 4 (x_hi: 2, x_lo: 2; x = x_hi * 2 + x_lo), y: 8, z: 16, core: 2. Of those that a mesh axis runs over, the one named last changes fastest.
Arguments:
- tokens: bfloat16 [196608, 4096], P(('rep', 'fsdp')), may hold values from -24 to 24
- quant_weight: bfloat16 [4096, 512], P('fsdp'), may hold values from -6 to 6
- block_scales: bfloat16 [1024], P('fsdp'), may hold values from 0.0069885254 to 0.031982422
- key_grad: bfloat16 [196608, 512], P(('rep', 'fsdp')), may hold values from -6 to 6
Outputs:
- rotated: bfloat16 [196608, 512], P(('rep', 'fsdp'))
- token_grad: bfloat16 [196608, 4096], P(('rep', 'fsdp'))
- weight_grad: bfloat16 [4096, 512], P(('rep', 'fsdp'))
The draws below stay inside these ranges and needn't reach their ends.
All inputs are finite; a program needn't handle non-finite values.
Results may differ from the reference program's by a relative error of at most 0.023.
Values may be sent and summed in bfloat16 or wider, within the bound.
No kernel may reach another device: no remote copies, remote signals or barrier semaphores. Data moves between devices by JAX's collectives and lax.ppermute only.
A program may use at most 64 MiB of HBM per device.

```python
import math
import jax
import jax.numpy as jnp
from jax import lax

DW = 4096
HEAD_DIM = 128
QBLOCK = 2048
TOK_DEV = 192
KVW = 512
TOKENS = 196608
N_REP = 32
N_FSDP = 32


def strengthened(result, rng, source, target, parts, factor):
    owner, partner = [(jnp.arange(result.shape[position]) // (result.shape[position] // parts)).reshape([-1 if axis == position else 1 for axis in range(result.ndim)]) for position in (source, target)]
    chosen = jax.random.permutation(rng, parts)[partner]
    strong = (owner == chosen) | (owner == (partner + parts // 2) % parts)
    return jnp.where(strong, factor * result, result)


def block_scale(key, shape, shards, low, high):
    def one(dim, parts):
        heights = jax.random.uniform(jax.random.fold_in(jax.random.fold_in(key, 6), dim), (parts,), jnp.float32, low / len(shards), high / len(shards))
        return jnp.repeat(jnp.exp(heights), shape[dim] // parts).reshape((-1,) + (1,) * (len(shape) - dim - 1))

    loudness = one(*shards[0])
    for cut in shards[1:]:
        loudness = loudness * one(*cut)
    return loudness


def bell_draw(key, extent, width, reach, shards=(), kind=jnp.bfloat16):
    result = jax.random.normal(key, extent, jnp.float32) * width
    if len(shards) > 0:
        result = block_scale(key, extent, shards, -0.22, 0.18) * result
    return jnp.clip(result, min=-reach, max=reach).astype(kind)


def noise_with(key, shape, spread, reach, split, heavy, held_as=jnp.bfloat16):
    result = spread * jax.random.normal(key, shape, jnp.float32)
    if split:
        result = result * block_scale(key, shape, split, -0.22, 0.18)
    return jnp.clip(strengthened(result, jax.random.fold_in(key, 3), *heavy), -reach, reach).astype(held_as)


def setup_inputs(seed: int = 0) -> dict:
    seeds = jax.random.split(jax.random.key(seed), 5)
    tokens = noise_with(seeds[0], (TOKENS, DW), 1.0, 24.0, ((0, 1024),), (0, 1, 1024, 6.0))
    quant_weight = bell_draw(seeds[1], (DW, KVW), 1.0, 6.0, ((0, 32),))
    block_scales = jnp.clip(jnp.exp(math.log(0.031982422) - 1.52091686 * jax.random.uniform(seeds[2], (DW * KVW // QBLOCK,), jnp.float32) ** block_scale(seeds[2], (DW * KVW // QBLOCK,), ((0, 32),), -0.2, 0.2)), 0.0069885254, 0.031982422).astype(jnp.bfloat16)
    key_grad = bell_draw(seeds[3], (TOKENS, KVW), 1.0, 6.0, ((0, 1024),))
    return {"tokens": tokens, "quant_weight": quant_weight, "block_scales": block_scales, "key_grad": key_grad}


rope_base = 10000.0

def dequantize(quant_weight, block_scales):
    rows_per_block = quant_weight.shape[0] // block_scales.shape[0]
    scaled = quant_weight.astype(jnp.float32).reshape(block_scales.shape[0], rows_per_block, quant_weight.shape[1])
    scaled = scaled * block_scales.astype(jnp.float32)[:, None, None]
    return scaled.reshape(quant_weight.shape).astype(jnp.bfloat16)

def rotary(projected, positions, direction):
    half_size = HEAD_DIM // 2
    steps = jnp.arange(half_size, dtype=jnp.int32).astype(jnp.float32)
    frequency = jnp.exp(steps * (-2.0 * math.log(rope_base) / HEAD_DIM))
    angles = positions[:, None] * frequency[None, :]
    cosine = jnp.cos(angles)[:, None, :]
    sine_part = direction * jnp.sin(angles)[:, None, :]
    halves = projected.reshape(projected.shape[0], -1, 2, half_size)
    leading = halves[:, :, 0]
    trailing = halves[:, :, 1]
    turned = jnp.stack([leading * cosine - trailing * sine_part, trailing * cosine + leading * sine_part], axis=2)
    return turned.reshape(projected.shape)

def reference(tokens, quant_weight, block_scales, key_grad):
    weight = dequantize(quant_weight, block_scales)
    device_count = N_REP * N_FSDP
    token_blocks = tokens.reshape(device_count, TOK_DEV, DW)
    grad_blocks = key_grad.reshape(device_count, TOK_DEV, KVW)
    offsets = jnp.arange(TOK_DEV, dtype=jnp.int32)

    def scan_step(running, inputs):
        token_block, key_block, device_index = inputs
        positions = (device_index % N_FSDP * TOK_DEV + offsets).astype(jnp.float32)
        projected = jnp.dot(token_block, weight, preferred_element_type=jnp.float32)
        rotated = rotary(projected, positions, 1.0).astype(jnp.bfloat16)
        proj_grad = rotary(key_block.astype(jnp.float32), positions, -1.0).astype(jnp.bfloat16)
        token_grad = jnp.dot(proj_grad, weight.T, preferred_element_type=jnp.float32).astype(jnp.bfloat16)
        partial_value = jnp.dot(token_block.T, proj_grad, preferred_element_type=jnp.float32).astype(jnp.bfloat16)
        partial_value = lax.optimization_barrier(partial_value)
        return (running + partial_value.astype(jnp.float32), (rotated, token_grad))
    start_sum = jnp.zeros((DW, KVW), jnp.float32)
    indices = jnp.arange(device_count, dtype=jnp.int32)
    summed, (rotated, token_grad) = lax.scan(scan_step, start_sum, (token_blocks, grad_blocks, indices))
    weight_grad = (summed * (1.0 / math.sqrt(TOKENS))).astype(jnp.bfloat16)
    return (rotated.reshape(TOKENS, KVW), token_grad.reshape(TOKENS, DW), weight_grad)
```

```python
import math

import jax
import jax.numpy as jnp
from jax import lax
from jax.experimental import pallas as pl
from jax.experimental.pallas import tpu as pltpu
from jax.sharding import Mesh
from jax.sharding import PartitionSpec as P

HEAD_DIM = 128
HALF = HEAD_DIM // 2
rope_base = 10000.0

SIZES = {"xl": 2, "zh": 8, "zl": 2, "xh": 2, "yh": 4, "yl": 2, "c": 2}
REP = ("xl", "zh", "zl")
FSDP = ("xh", "yh", "yl", "c")
NEAR = ("xl", "zl", "xh", "yl")
FAR = ("zh", "yh")
SWAP = [(0, 1), (1, 0)]


def dequantize(quant_weight, block_scales):
    rows_per_block = quant_weight.shape[0] // block_scales.shape[0]
    scaled = quant_weight.astype(jnp.float32).reshape(
        block_scales.shape[0], rows_per_block, quant_weight.shape[1]
    )
    scaled = scaled * block_scales.astype(jnp.float32)[:, None, None]
    return scaled.reshape(quant_weight.shape).astype(jnp.bfloat16)


def tables(positions):
    steps = jnp.arange(HALF, dtype=jnp.int32).astype(jnp.float32)
    frequency = jnp.exp(steps * (-2.0 * math.log(rope_base) / HEAD_DIM))
    angles = positions.astype(jnp.float32)[:, None] * frequency[None, :]
    cosine, sine = jnp.cos(angles), jnp.sin(angles)
    return jnp.concatenate([cosine, cosine], 1), jnp.concatenate([-sine, sine], 1)


def turn(values, cosine, sine, heads):
    parts = []
    for h in range(heads):
        part = values[:, h * HEAD_DIM : (h + 1) * HEAD_DIM]
        parts.append(part * cosine + pltpu.roll(part, HALF, 1) * sine)
    return parts


def grad_kernel(own, other, kg_own, kg_other, cos, sin, pick, out, proj_grad):
    rows = own.shape[0]
    heads = kg_own.shape[1] // HEAD_DIM

    @pl.when(pl.program_id(0) == 0)
    def _():
        for k, source in enumerate((kg_own, kg_other)):
            at = pl.ds(k * rows, rows)
            parts = turn(source[...].astype(jnp.float32), cos[at, :], -sin[at, :], heads)
            for h, part in enumerate(parts):
                proj_grad[at, h * HEAD_DIM : (h + 1) * HEAD_DIM] = part.astype(jnp.bfloat16)

    wide = pick.shape[1]
    for b in range(own.shape[1] // wide):
        at = slice(b * wide, (b + 1) * wide)
        chunk = jnp.concatenate([own[:, at], other[:, at]], 0)
        picked = lax.dot_general(
            pick[...], chunk, (((1,), (1,)), ((), ())), preferred_element_type=jnp.float32
        ).astype(jnp.bfloat16)
        partial = jnp.dot(picked, proj_grad[...], preferred_element_type=jnp.float32)
        partial = partial.astype(jnp.bfloat16)
        for k in range(8):
            out[0, k, b] = partial[k * 16 : (k + 1) * 16]


def weight_partial(own, other, kg_own, kg_other, cos, sin, pick):
    rows, features = own.shape
    kvw = kg_own.shape[1]
    blocks = 4
    width = features // 4
    whole = lambda a: pl.BlockSpec(a.shape, lambda s: (0, 0))
    return pl.pallas_call(
        grad_kernel,
        grid=(4,),
        out_shape=jax.ShapeDtypeStruct((2, 8, 8, 16, kvw), jnp.bfloat16),
        in_specs=[
            pl.BlockSpec((rows, width), lambda s: (0, s)),
            pl.BlockSpec((rows, width), lambda s: (0, s)),
            whole(kg_own),
            whole(kg_other),
            whole(cos),
            whole(sin),
            whole(pick),
        ],
        out_specs=pl.BlockSpec((1, 8, blocks, 16, kvw), lambda s: (s // 2, 0, s % 2, 0, 0)),
        scratch_shapes=[pltpu.VMEM((2 * rows, kvw), jnp.bfloat16)],
        compiler_params=pltpu.CompilerParams(vmem_limit_bytes=32 * 2**20),
        cost_estimate=pl.CostEstimate(
            flops=6 * rows * features * kvw // 2, bytes_accessed=6 * 2**20, transcendentals=0
        ),
        name="weight_partial",
    )(own, other, kg_own, kg_other, cos, sin, pick)


def forward_kernel(core, tokens, key_grad, cos, sin, w_own, w_other, rotated, token_grad, weight, sems):
    heads = key_grad.shape[1] // HEAD_DIM
    c = core[0]
    copies = []
    for y in range(8):
        pair = [
            pltpu.make_async_copy(w_own.at[y], weight.at[:, y, c], sems.at[0, y]),
            pltpu.make_async_copy(w_other.at[y], weight.at[:, y, 1 - c], sems.at[1, y]),
        ]
        for copy in pair:
            copy.start()
        copies.append(pair)
    cosine, sine = cos[...], sin[...]
    parts = turn(key_grad[...].astype(jnp.float32), cosine, -sine, heads)
    proj_grad = jnp.concatenate([p.astype(jnp.bfloat16) for p in parts], 1)
    projected = jnp.zeros(key_grad.shape, jnp.float32)
    for y in range(8):
        for copy in copies[y]:
            copy.wait()
        for xh in range(2):
            at = slice((xh * 8 + y) * 256, (xh * 8 + y + 1) * 256)
            block = weight[xh, y].reshape(256, key_grad.shape[1])
            projected = projected + jnp.dot(
                tokens[:, at], block, preferred_element_type=jnp.float32
            )
            token_grad[:, at] = lax.dot_general(
                proj_grad, block, (((1,), (1,)), ((), ())), preferred_element_type=jnp.float32
            ).astype(jnp.bfloat16)
    for h, part in enumerate(turn(projected, cosine, sine, heads)):
        rotated[:, h * HEAD_DIM : (h + 1) * HEAD_DIM] = part.astype(jnp.bfloat16)


def forward(core, tokens, key_grad, cos, sin, w_own, w_other):
    rows, features = tokens.shape
    kvw = key_grad.shape[1]
    vmem = pl.BlockSpec(memory_space=pltpu.VMEM)
    return pl.pallas_call(
        forward_kernel,
        out_shape=(
            jax.ShapeDtypeStruct((rows, kvw), jnp.bfloat16),
            jax.ShapeDtypeStruct((rows, features), jnp.bfloat16),
        ),
        in_specs=[pl.BlockSpec(memory_space=pltpu.SMEM)]
        + [vmem] * 4
        + [pl.BlockSpec(memory_space=pl.ANY)] * 2,
        out_specs=(vmem, vmem),
        scratch_shapes=[
            pltpu.VMEM((2, 8, 2, 128, kvw), jnp.bfloat16),
            pltpu.SemaphoreType.DMA((2, 8)),
        ],
        compiler_params=pltpu.CompilerParams(vmem_limit_bytes=32 * 2**20),
        cost_estimate=pl.CostEstimate(
            flops=4 * rows * features * kvw, bytes_accessed=8 * 2**20, transcendentals=0
        ),
        name="forward",
    )(core, tokens, key_grad, cos, sin, w_own, w_other)


def pick_matrix(core):
    q = lax.broadcasted_iota(jnp.int32, (128, 256), 0)
    lane = lax.broadcasted_iota(jnp.int32, (128, 256), 1)
    zl_xh, yl, yh, j = q // 32, q // 16 % 2, q // 4 % 4, q % 4
    return (lane == zl_xh * 64 + yh * 16 + yl * 8 + core * 4 + j).astype(jnp.bfloat16)


def body(tokens, quant_weight, block_scales, key_grad):
    rows = tokens.shape[0]
    kvw = key_grad.shape[1]
    core = lax.axis_index("c")
    xh = lax.axis_index("xh")
    place = lax.axis_index(FSDP)

    other_tokens = lax.ppermute(tokens, "c", SWAP)
    other_key_grad = lax.ppermute(key_grad, "c", SWAP)

    shard = dequantize(quant_weight, block_scales)
    across = lax.ppermute(shard, ("xl", "xh"), [(i, 3 - i) for i in range(4)])
    both = jnp.where(xh == 0, jnp.stack([shard, across]), jnp.stack([across, shard]))
    w_own = lax.all_gather(both, ("yh", "yl"), axis=0)

    offsets = jnp.arange(rows, dtype=jnp.int32)
    positions = jnp.concatenate([place * rows + offsets, (place + 1 - 2 * core) * rows + offsets])
    cos, sin = tables(positions)

    partial = weight_partial(
        tokens, other_tokens, key_grad, other_key_grad, cos, sin, pick_matrix(core)
    )
    near = lax.all_to_all(partial.reshape(16, 128, kvw), NEAR, 0, 0)
    near_sum = near.astype(jnp.float32).sum(0).astype(jnp.bfloat16)
    far = lax.all_to_all(near_sum.reshape(32, 4, kvw), FAR, 0, 0)
    summed = far.astype(jnp.float32).sum(0)
    count = rows * math.prod(SIZES.values())
    weight_grad = (summed * (1.0 / math.sqrt(count))).astype(jnp.bfloat16)

    w_other = lax.ppermute(w_own, "c", SWAP)
    rotated, token_grad = forward(
        core.reshape(1), tokens, key_grad, cos[:rows], sin[:rows], w_own, w_other
    )
    return (rotated, token_grad, weight_grad)


def solution(mesh):
    fine = Mesh(mesh.devices.reshape(tuple(SIZES.values())), tuple(SIZES))
    everywhere = P(REP + FSDP, None)
    return jax.shard_map(
        body,
        mesh=fine,
        in_specs=(everywhere, P(FSDP, None), P(FSDP), everywhere),
        out_specs=(everywhere, everywhere, everywhere),
        check_vma=False,
    )
```

```python
import math

import jax
import jax.numpy as jnp
from jax import lax
from jax.experimental import pallas as pl
from jax.experimental.pallas import tpu as pltpu
from jax.sharding import Mesh
from jax.sharding import PartitionSpec as P

HEAD_DIM = 128
HALF = HEAD_DIM // 2
rope_base = 10000.0

SIZES = {"xl": 2, "zh": 8, "zl": 2, "xh": 2, "yh": 4, "yl": 2, "c": 2}
REP = ("xl", "zh", "zl")
FSDP = ("xh", "yh", "yl", "c")
NEAR = ("xl", "zl", "xh", "c")
FAR = ("zh", "yh", "yl")
SWAP = [(0, 1), (1, 0)]
GRANT = 32 * 2**20
QUICK = pl.CostEstimate(flops=0, bytes_accessed=0, transcendentals=0)


def dequantize_kernel(scales, quant, out):
    rows, groups = quant.shape[0], scales.shape[1]
    group = lax.broadcasted_iota(jnp.int32, (rows, groups), 0) // (rows // groups)
    lane = lax.broadcasted_iota(jnp.int32, (rows, groups), 1)
    spread = jnp.where(group == lane, scales[...].astype(jnp.float32), 0.0)
    scale = jnp.sum(spread, axis=1, keepdims=True)
    out[...] = (quant[...].astype(jnp.float32) * scale).astype(jnp.bfloat16)


def dequantize(quant_weight, block_scales):
    return pl.pallas_call(
        dequantize_kernel,
        out_shape=jax.ShapeDtypeStruct(quant_weight.shape, jnp.bfloat16),
        name="dequantize",
    )(block_scales.reshape(1, -1), quant_weight)


def pair_kernel(xh, own, across, out):
    out[xh[0]] = own[...]
    out[1 - xh[0]] = across[...]


def pair(xh, own, across):
    vmem = pl.BlockSpec(memory_space=pltpu.VMEM)
    return pl.pallas_call(
        pair_kernel,
        out_shape=jax.ShapeDtypeStruct((2,) + own.shape, own.dtype),
        in_specs=[pl.BlockSpec(memory_space=pltpu.SMEM), vmem, vmem],
        out_specs=vmem,
        name="pair",
    )(xh.reshape(1), own, across)


def gather(across_xh):
    right = [(i, (i + 1) % 8) for i in range(8)]
    left = [(i, (i + 7) % 8) for i in range(8)]
    axes = ("yh", "yl")
    rights, lefts = [across_xh], [across_xh]
    for _ in range(3):
        rights.append(lax.ppermute(rights[-1], axes, right))
        lefts.append(lax.ppermute(lefts[-1], axes, left))
    rights.append(lax.ppermute(rights[-1], axes, right))
    return rights + lefts[1:]


def near_kernel(near, after_right, after_left, out):
    chips, cores, rows, width = near.shape
    for r in range(0, rows, 16):
        at = slice(r, r + 16)
        for c in range(cores):
            total = near[0, c, at].astype(jnp.float32)
            for chip in range(1, chips):
                total = total + near[chip, c, at].astype(jnp.float32)
            out[at, c * width : (c + 1) * width] = total.astype(jnp.bfloat16)


def near_total(near, after_right, after_left):
    chips, cores, rows, width = near.shape
    vmem = pl.BlockSpec(memory_space=pltpu.VMEM)
    anywhere = pl.BlockSpec(memory_space=pl.ANY)
    return pl.pallas_call(
        near_kernel,
        out_shape=jax.ShapeDtypeStruct((rows, cores * width), jnp.bfloat16),
        in_specs=[vmem, anywhere, anywhere],
        out_specs=vmem,
        compiler_params=pltpu.CompilerParams(vmem_limit_bytes=GRANT),
        cost_estimate=QUICK,
        name="near_total",
    )(near, after_right, after_left)


def tables(positions):
    lane = jnp.arange(HEAD_DIM, dtype=jnp.int32)
    steps = (lane % HALF).astype(jnp.float32)
    frequency = jnp.exp(steps * (-2.0 * math.log(rope_base) / HEAD_DIM))
    angles = positions.astype(jnp.float32)[:, None] * frequency[None, :]
    sign = jnp.where(lane < HALF, -1.0, 1.0)[None, :]
    return jnp.cos(angles), sign * jnp.sin(angles)


def turn(values, cosine, sine, heads):
    parts = []
    for h in range(heads):
        part = values[:, h * HEAD_DIM : (h + 1) * HEAD_DIM]
        parts.append(part * cosine + pltpu.roll(part, HALF, 1) * sine)
    return parts


def grad_kernel(core, own, other, kg_own, kg_other, cos, sin, after, out, proj_grad):
    rows, features = own.shape
    width = proj_grad.shape[1]
    mine = pl.multiple_of(core[0] * width, width)
    for k, source in enumerate((kg_own, kg_other)):
        at = pl.ds(k * rows, rows)
        values = source[:, pl.ds(mine, width)].astype(jnp.float32)
        parts = turn(values, cos[at, :], -sin[at, :], width // HEAD_DIM)
        for h, part in enumerate(parts):
            proj_grad[at, h * HEAD_DIM : (h + 1) * HEAD_DIM] = part.astype(jnp.bfloat16)

    low = lax.broadcasted_iota(jnp.int32, (8, width), 0) < 4
    for block in range(features // 256):
        at = slice(block * 256, (block + 1) * 256)
        partial = lax.dot_general(
            jnp.concatenate([own[:, at], other[:, at]], 0),
            proj_grad[...],
            (((0,), (0,)), ((), ())),
            preferred_element_type=jnp.float32,
        )
        xl, zh = divmod(block, 8)
        for k in range(4):
            first, second = [], []
            for y in range(0, 8, 2):
                start = k * 64 + y * 8
                even, odd = partial[start : start + 8], partial[start + 8 : start + 16]
                first.append(jnp.where(low, even, pltpu.roll(odd, 4, 0)))
                second.append(jnp.where(low, pltpu.roll(even, 4, 0), odd))
            out[xl, k, 0, zh] = jnp.concatenate(first, 0).astype(jnp.bfloat16)
            out[xl, k, 1, zh] = jnp.concatenate(second, 0).astype(jnp.bfloat16)


def weight_partial(core, own, other, kg_own, kg_other, cos, sin, after):
    rows, features = own.shape
    kvw = kg_own.shape[1]
    vmem = pl.BlockSpec(memory_space=pltpu.VMEM)
    return pl.pallas_call(
        grad_kernel,
        out_shape=jax.ShapeDtypeStruct((2, 4, 2, 8, 32, kvw // 2), jnp.bfloat16),
        in_specs=[pl.BlockSpec(memory_space=pltpu.SMEM)]
        + [vmem] * 6
        + [pl.BlockSpec(memory_space=pl.ANY)],
        out_specs=vmem,
        scratch_shapes=[pltpu.VMEM((2 * rows, kvw // 2), jnp.bfloat16)],
        compiler_params=pltpu.CompilerParams(vmem_limit_bytes=GRANT),
        cost_estimate=QUICK,
        name="weight_partial",
    )(core, own, other, kg_own, kg_other, cos, sin, after)


def forward_kernel(
    place, own, other, kg_own, kg_other, cos, sin, *refs
):
    blocks, (after, p_own, p_other, t_own, t_other, proj_grad, total) = refs[:8], refs[8:]
    rows, kvw = kg_own.shape
    core, y = place[0], place[1]
    for k, source in enumerate((kg_own, kg_other)):
        at = pl.ds(k * rows, rows)
        parts = turn(source[...].astype(jnp.float32), cos[at, :], -sin[at, :], kvw // HEAD_DIM)
        for h, part in enumerate(parts):
            proj_grad[at, h * HEAD_DIM : (h + 1) * HEAD_DIM] = part.astype(jnp.bfloat16)
    for k, block in enumerate(blocks):
        there = lax.rem(y + (8 - k if k <= 4 else k - 4), 8)
        weight = block[...].reshape(256, kvw)
        taken = []
        for source in (own, other):
            halves = [
                source[:, pl.ds(pl.multiple_of((xh * 8 + there) * 256 + core * 128, 128), 128)]
                for xh in range(2)
            ]
            taken.append(jnp.concatenate(halves, 1))
        share = jnp.dot(jnp.concatenate(taken, 0), weight, preferred_element_type=jnp.float32)
        total[...] = share if k == 0 else total[...] + share
        back = lax.dot_general(
            proj_grad[...], weight, (((1,), (1,)), ((), ())), preferred_element_type=jnp.float32
        ).astype(jnp.bfloat16)
        for xh in range(2):
            at = pl.ds(pl.multiple_of((xh * 8 + there) * 128, 128), 128)
            t_own[:, at] = back[:rows, xh * 128 : (xh + 1) * 128]
            t_other[:, at] = back[rows:, xh * 128 : (xh + 1) * 128]
    p_own[...] = total[:rows]
    p_other[...] = total[rows:]


def forward(place, own, other, kg_own, kg_other, cos, sin, blocks, after):
    rows, features = own.shape
    kvw = kg_own.shape[1]
    vmem = pl.BlockSpec(memory_space=pltpu.VMEM)
    return pl.pallas_call(
        forward_kernel,
        out_shape=[jax.ShapeDtypeStruct((rows, kvw), jnp.float32)] * 2
        + [jax.ShapeDtypeStruct((rows, features // 2), jnp.bfloat16)] * 2,
        in_specs=[pl.BlockSpec(memory_space=pltpu.SMEM)]
        + [vmem] * 14
        + [pl.BlockSpec(memory_space=pl.ANY)],
        out_specs=[vmem] * 4,
        scratch_shapes=[
            pltpu.VMEM((2 * rows, kvw), jnp.bfloat16),
            pltpu.VMEM((2 * rows, kvw), jnp.float32),
        ],
        compiler_params=pltpu.CompilerParams(vmem_limit_bytes=GRANT),
        cost_estimate=QUICK,
        name="forward",
    )(place, own, other, kg_own, kg_other, cos, sin, *blocks, after)


def finish_kernel(core, p_own, p_other, t_own, t_other, cos, sin, rotated, token_grad):
    kvw = p_own.shape[1]
    total = p_own[...] + p_other[...]
    for h, part in enumerate(turn(total, cos[...], sin[...], kvw // HEAD_DIM)):
        rotated[:, h * HEAD_DIM : (h + 1) * HEAD_DIM] = part.astype(jnp.bfloat16)
    for f in range(t_own.shape[1] // 128):
        at = slice(f * 128, (f + 1) * 128)
        for source, parity in ((t_own, core[0]), (t_other, 1 - core[0])):
            column = pl.multiple_of(f * 256 + parity * 128, 128)
            token_grad[:, pl.ds(column, 128)] = source[:, at]


def finish(core, p_own, p_other, t_own, t_other, cos, sin):
    rows, kvw = p_own.shape
    features = 2 * t_own.shape[1]
    steps = 3
    block = lambda width: pl.BlockSpec((rows // steps, width), lambda s: (s, 0))
    return pl.pallas_call(
        finish_kernel,
        grid=(steps,),
        out_shape=(
            jax.ShapeDtypeStruct((rows, kvw), jnp.bfloat16),
            jax.ShapeDtypeStruct((rows, features), jnp.bfloat16),
        ),
        in_specs=[pl.BlockSpec(memory_space=pltpu.SMEM)]
        + [block(kvw)] * 2
        + [block(features // 2)] * 2
        + [block(HEAD_DIM)] * 2,
        out_specs=(block(kvw), block(features)),
        compiler_params=pltpu.CompilerParams(vmem_limit_bytes=GRANT),
        cost_estimate=QUICK,
        name="finish",
    )(core, p_own, p_other, t_own, t_other, cos, sin)


def body(tokens, quant_weight, block_scales, key_grad):
    rows = tokens.shape[0]
    kvw = key_grad.shape[1]
    core = lax.axis_index("c")
    xh = lax.axis_index("xh")
    place = lax.axis_index(FSDP)

    shard = dequantize(quant_weight, block_scales)
    across = lax.ppermute(shard, ("xl", "xh"), [(i, 3 - i) for i in range(4)])
    both = pair(xh, shard, across)
    blocks = gather(both)

    other_tokens = lax.ppermute(tokens, "c", SWAP)
    other_key_grad = lax.ppermute(key_grad, "c", SWAP)

    offsets = jnp.arange(rows, dtype=jnp.int32)
    positions = jnp.concatenate([place * rows + offsets, (place + 1 - 2 * core) * rows + offsets])
    cos, sin = tables(positions)

    partial = weight_partial(
        core.reshape(1), tokens, other_tokens, key_grad, other_key_grad, cos, sin, both
    )
    near = lax.all_to_all(partial.reshape(16, 256, kvw // 2), NEAR, 0, 0)
    near_sum = near_total(near.reshape(8, 2, 256, kvw // 2), blocks[3], blocks[7])
    far = lax.all_to_all(near_sum, FAR, 0, 0, tiled=True)
    summed = far.reshape(64, 4, kvw).astype(jnp.float32).sum(0)
    count = rows * math.prod(SIZES.values())
    weight_grad = (summed * (1.0 / math.sqrt(count))).astype(jnp.bfloat16)

    y = lax.axis_index(("yh", "yl"))
    p_own, p_other, t_own, t_other = forward(
        jnp.stack([core, y]),
        tokens,
        other_tokens,
        key_grad,
        other_key_grad,
        cos,
        sin,
        blocks,
        near_sum,
    )
    p_other = lax.ppermute(p_other, "c", SWAP)
    t_other = lax.ppermute(t_other, "c", SWAP)
    rotated, token_grad = finish(core.reshape(1), p_own, p_other, t_own, t_other, cos, sin)
    return (rotated, token_grad, weight_grad)


def solution(mesh):
    fine = Mesh(mesh.devices.reshape(tuple(SIZES.values())), tuple(SIZES))
    everywhere = P(REP + FSDP, None)
    return jax.shard_map(
        body,
        mesh=fine,
        in_specs=(everywhere, P(FSDP, None), P(FSDP), everywhere),
        out_specs=(everywhere, everywhere, everywhere),
        check_vma=False,
    )
```

```python
import math

import jax
import jax.numpy as jnp
from jax import lax
from jax.experimental import pallas as pl
from jax.experimental.pallas import tpu as pltpu
from jax.sharding import Mesh
from jax.sharding import PartitionSpec as P

HEAD_DIM = 128
HALF = HEAD_DIM // 2
rope_base = 10000.0

SIZES = {"xl": 2, "zh": 8, "zl": 2, "xh": 2, "yh": 4, "yl": 2, "c": 2}
REP = ("xl", "zh", "zl")
FSDP = ("xh", "yh", "yl", "c")
NEAR = ("xl", "zl", "xh", "c")
FAR = ("zh", "yh", "yl")
SWAP = [(0, 1), (1, 0)]
GRANT = 8 * 2**20
WIDE = 56 * 2**20
QUICK = pl.CostEstimate(flops=0, bytes_accessed=0, transcendentals=0)


def dequantize_kernel(scales, quant, out):
    rows, groups = quant.shape[0], scales.shape[1]
    group = lax.broadcasted_iota(jnp.int32, (rows, groups), 0) // (rows // groups)
    lane = lax.broadcasted_iota(jnp.int32, (rows, groups), 1)
    spread = jnp.where(group == lane, scales[...].astype(jnp.float32), 0.0)
    scale = jnp.sum(spread, axis=1, keepdims=True)
    out[...] = (quant[...].astype(jnp.float32) * scale).astype(jnp.bfloat16)


def dequantize(quant_weight, block_scales):
    return pl.pallas_call(
        dequantize_kernel,
        out_shape=jax.ShapeDtypeStruct(quant_weight.shape, jnp.bfloat16),
        compiler_params=pltpu.CompilerParams(vmem_limit_bytes=GRANT),
        cost_estimate=QUICK,
        name="dequantize",
    )(block_scales.reshape(1, -1), quant_weight)


def pair_kernel(here, own, across, passed, out, passed_on):
    out[here[0]] = own[...]
    out[1 - here[0]] = across[...]


def pair(here, own, across, passed):
    vmem = pl.BlockSpec(memory_space=pltpu.VMEM)
    anywhere = pl.BlockSpec(memory_space=pl.ANY)
    return pl.pallas_call(
        pair_kernel,
        out_shape=(
            jax.ShapeDtypeStruct((2,) + own.shape, own.dtype),
            jax.ShapeDtypeStruct(passed.shape, passed.dtype),
        ),
        in_specs=[pl.BlockSpec(memory_space=pltpu.SMEM), vmem, vmem, anywhere],
        out_specs=(vmem, anywhere),
        input_output_aliases={3: 1},
        compiler_params=pltpu.CompilerParams(vmem_limit_bytes=GRANT),
        cost_estimate=QUICK,
        name="pair",
    )(here, own, across, passed)


def gather(across_xh):
    right = [(i, (i + 1) % 8) for i in range(8)]
    left = [(i, (i + 7) % 8) for i in range(8)]
    axes = ("yh", "yl")
    rights, lefts = [across_xh], [across_xh]
    for _ in range(3):
        rights.append(lax.ppermute(rights[-1], axes, right))
        lefts.append(lax.ppermute(lefts[-1], axes, left))
    rights.append(lax.ppermute(rights[-1], axes, right))
    return rights + lefts[1:]


def near_kernel(near, after_right, after_left, out):
    chips, cores, rows, width = near.shape
    for r in range(0, rows, 16):
        at = slice(r, r + 16)
        for c in range(cores):
            total = near[0, c, at].astype(jnp.float32)
            for chip in range(1, chips):
                total = total + near[chip, c, at].astype(jnp.float32)
            out[at, c * width : (c + 1) * width] = total.astype(jnp.bfloat16)


def near_total(near, after_right, after_left):
    chips, cores, rows, width = near.shape
    vmem = pl.BlockSpec(memory_space=pltpu.VMEM)
    anywhere = pl.BlockSpec(memory_space=pl.ANY)
    return pl.pallas_call(
        near_kernel,
        out_shape=jax.ShapeDtypeStruct((rows, cores * width), jnp.bfloat16),
        in_specs=[vmem, anywhere, anywhere],
        out_specs=vmem,
        compiler_params=pltpu.CompilerParams(vmem_limit_bytes=GRANT),
        cost_estimate=QUICK,
        name="near_total",
    )(near, after_right, after_left)


def tables(positions):
    lane = jnp.arange(HEAD_DIM, dtype=jnp.int32)
    steps = (lane % HALF).astype(jnp.float32)
    frequency = jnp.exp(steps * (-2.0 * math.log(rope_base) / HEAD_DIM))
    angles = positions.astype(jnp.float32)[:, None] * frequency[None, :]
    sign = jnp.where(lane < HALF, -1.0, 1.0)[None, :]
    return jnp.cos(angles), sign * jnp.sin(angles)


def turn(values, cosine, sine, heads):
    parts = []
    for h in range(heads):
        part = values[:, h * HEAD_DIM : (h + 1) * HEAD_DIM]
        parts.append(part * cosine + pltpu.roll(part, HALF, 1) * sine)
    return parts


def grad_kernel(core, own, other, kg_own, kg_other, cos, sin, out, proj_grad):
    rows, features = own.shape
    width = proj_grad.shape[1]
    mine = pl.multiple_of(core[0] * width, width)
    for k, source in enumerate((kg_own, kg_other)):
        at = pl.ds(k * rows, rows)
        values = source[:, pl.ds(mine, width)].astype(jnp.float32)
        parts = turn(values, cos[at, :], -sin[at, :], width // HEAD_DIM)
        for h, part in enumerate(parts):
            proj_grad[at, h * HEAD_DIM : (h + 1) * HEAD_DIM] = part.astype(jnp.bfloat16)

    low = lax.broadcasted_iota(jnp.int32, (8, width), 0) < 4
    for block in range(features // 256):
        at = slice(block * 256, (block + 1) * 256)
        partial = lax.dot_general(
            jnp.concatenate([own[:, at], other[:, at]], 0),
            proj_grad[...],
            (((0,), (0,)), ((), ())),
            preferred_element_type=jnp.float32,
        )
        xl, zh = divmod(block, 8)
        for k in range(4):
            first, second = [], []
            for y in range(0, 8, 2):
                start = k * 64 + y * 8
                even, odd = partial[start : start + 8], partial[start + 8 : start + 16]
                first.append(jnp.where(low, even, pltpu.roll(odd, 4, 0)))
                second.append(jnp.where(low, pltpu.roll(even, 4, 0), odd))
            out[xl, k, 0, zh] = jnp.concatenate(first, 0).astype(jnp.bfloat16)
            out[xl, k, 1, zh] = jnp.concatenate(second, 0).astype(jnp.bfloat16)


def weight_partial(core, own, other, kg_own, kg_other, cos, sin):
    rows, features = own.shape
    kvw = kg_own.shape[1]
    vmem = pl.BlockSpec(memory_space=pltpu.VMEM)
    return pl.pallas_call(
        grad_kernel,
        out_shape=jax.ShapeDtypeStruct((2, 4, 2, 8, 32, kvw // 2), jnp.bfloat16),
        in_specs=[pl.BlockSpec(memory_space=pltpu.SMEM)] + [vmem] * 6,
        out_specs=vmem,
        scratch_shapes=[pltpu.VMEM((2 * rows, kvw // 2), jnp.bfloat16)],
        compiler_params=pltpu.CompilerParams(vmem_limit_bytes=GRANT),
        cost_estimate=pl.CostEstimate(
            flops=2 * rows * features * kvw, bytes_accessed=8 * 2**20, transcendentals=0
        ),
        name="weight_partial",
    )(core, own, other, kg_own, kg_other, cos, sin)


def forward_kernel(place, own, other, kg_own, kg_other, cos, sin, *refs):
    blocks, (after, p_out, t_out, p_sent, t_sent) = refs[:8], refs[8:13]
    t_own, t_other, held, kg, weights, proj_grad, total, sems = refs[13:]
    rows, kvw = kg_own.shape
    core, y = place[0], place[1]
    part = rows // 4
    pairs = [(kg_own, kg.at[pl.ds(0, rows)]), (kg_other, kg.at[pl.ds(rows, rows)])]
    pairs += [(block, weights.at[k]) for k, block in enumerate(blocks)]
    pairs += [
        (source.at[pl.ds(q * part, part)], held.at[pl.ds(k * rows + q * part, part)])
        for k, source in enumerate((own, other))
        for q in range(4)
    ]
    loads = [pltpu.make_async_copy(a, b, sems.at[i]) for i, (a, b) in enumerate(pairs)]
    for copy in loads:
        copy.start()
    for k in range(2):
        at = pl.ds(k * rows, rows)
        loads[k].wait()
        parts = turn(kg[at, :].astype(jnp.float32), cos[at, :], -sin[at, :], kvw // HEAD_DIM)
        for h, p in enumerate(parts):
            proj_grad[at, h * HEAD_DIM : (h + 1) * HEAD_DIM] = p.astype(jnp.bfloat16)

    def column(k, xh):
        return xh * 8 + lax.rem(y + (8 - k if k <= 4 else k - 4), 8)

    for k in range(8):
        loads[2 + k].wait()
        back = lax.dot_general(
            proj_grad[...],
            weights[k].reshape(256, kvw),
            (((1,), (1,)), ((), ())),
            preferred_element_type=jnp.float32,
        ).astype(jnp.bfloat16)
        for xh in range(2):
            at = pl.ds(pl.multiple_of(column(k, xh) * 128, 128), 128)
            half = slice(xh * 128, (xh + 1) * 128)
            t_own[:, at] = back[:rows, half]
            t_other[:, at] = back[rows:, half]
    stores = [
        pltpu.make_async_copy(t_other, t_sent, sems.at[0]),
        pltpu.make_async_copy(t_own, t_out, sems.at[1]),
        pltpu.make_async_copy(total.at[pl.ds(rows, rows)], p_sent, sems.at[2]),
        pltpu.make_async_copy(total.at[pl.ds(0, rows)], p_out, sems.at[3]),
    ]
    for store in stores[:2]:
        store.start()
    for copy in loads[10:]:
        copy.wait()
    for k in range(8):
        taken = [
            held[:, pl.ds(pl.multiple_of(column(k, xh) * 256 + core * 128, 128), 128)]
            for xh in range(2)
        ]
        share = jnp.dot(
            jnp.concatenate(taken, 1),
            weights[k].reshape(256, kvw),
            preferred_element_type=jnp.float32,
        )
        total[...] = share if k == 0 else total[...] + share
    for store in stores[2:]:
        store.start()
    for copy in stores:
        copy.wait()


def forward(place, own, other, kg_own, kg_other, cos, sin, blocks, after):
    rows, features = own.shape
    kvw = kg_own.shape[1]
    vmem = pl.BlockSpec(memory_space=pltpu.VMEM)
    anywhere = pl.BlockSpec(memory_space=pl.ANY)
    return pl.pallas_call(
        forward_kernel,
        out_shape=(
            jax.ShapeDtypeStruct((rows, kvw), jnp.float32),
            jax.ShapeDtypeStruct((rows, features // 2), jnp.bfloat16),
            jax.ShapeDtypeStruct((rows, kvw), jnp.float32),
            jax.ShapeDtypeStruct((rows, features // 2), jnp.bfloat16),
        ),
        in_specs=[pl.BlockSpec(memory_space=pltpu.SMEM)]
        + [anywhere] * 4
        + [vmem] * 2
        + [anywhere] * 9,
        out_specs=[anywhere] * 4,
        scratch_shapes=[
            pltpu.VMEM((rows, features // 2), jnp.bfloat16),
            pltpu.VMEM((rows, features // 2), jnp.bfloat16),
            pltpu.VMEM((2 * rows, features), jnp.bfloat16),
            pltpu.VMEM((2 * rows, kvw), jnp.bfloat16),
            pltpu.VMEM((8,) + blocks[0].shape, jnp.bfloat16),
            pltpu.VMEM((2 * rows, kvw), jnp.bfloat16),
            pltpu.VMEM((2 * rows, kvw), jnp.float32),
            pltpu.SemaphoreType.DMA((18,)),
        ],
        compiler_params=pltpu.CompilerParams(vmem_limit_bytes=WIDE),
        cost_estimate=QUICK,
        name="forward",
    )(place, own, other, kg_own, kg_other, cos, sin, *blocks, after)


def finish_kernel(core, p_own, t_own, p_other, t_other, cos, sin, rotated, token_grad):
    kvw = p_own.shape[1]
    total = p_own[...] + p_other[...]
    for h, part in enumerate(turn(total, cos[...], sin[...], kvw // HEAD_DIM)):
        rotated[:, h * HEAD_DIM : (h + 1) * HEAD_DIM] = part.astype(jnp.bfloat16)
    for f in range(t_own.shape[1] // 128):
        at = slice(f * 128, (f + 1) * 128)
        for source, parity in ((t_own, core[0]), (t_other, 1 - core[0])):
            column = pl.multiple_of(f * 256 + parity * 128, 128)
            token_grad[:, pl.ds(column, 128)] = source[:, at]


def finish(core, p_own, t_own, p_other, t_other, cos, sin):
    rows, kvw = p_own.shape
    features = 2 * t_own.shape[1]
    steps = 3
    block = lambda width: pl.BlockSpec((rows // steps, width), lambda s: (s, 0))
    return pl.pallas_call(
        finish_kernel,
        grid=(steps,),
        out_shape=(
            jax.ShapeDtypeStruct((rows, kvw), jnp.bfloat16),
            jax.ShapeDtypeStruct((rows, features), jnp.bfloat16),
        ),
        in_specs=[pl.BlockSpec(memory_space=pltpu.SMEM)]
        + [block(kvw), block(features // 2)] * 2
        + [block(HEAD_DIM)] * 2,
        out_specs=(block(kvw), block(features)),
        compiler_params=pltpu.CompilerParams(vmem_limit_bytes=WIDE),
        cost_estimate=QUICK,
        name="finish",
    )(core, p_own, t_own, p_other, t_other, cos, sin)


def body(tokens, quant_weight, block_scales, key_grad):
    rows = tokens.shape[0]
    kvw = key_grad.shape[1]
    core = lax.axis_index("c")
    xh = lax.axis_index("xh")
    place = lax.axis_index(FSDP)

    shard = dequantize(quant_weight, block_scales)
    across = lax.ppermute(shard, ("xl", "xh"), [(i, 3 - i) for i in range(4)])
    other_tokens = lax.ppermute(tokens, "c", SWAP)
    other_key_grad = lax.ppermute(key_grad, "c", SWAP)

    offsets = jnp.arange(rows, dtype=jnp.int32)
    positions = jnp.concatenate([place * rows + offsets, (place + 1 - 2 * core) * rows + offsets])
    cos, sin = tables(positions)

    partial = weight_partial(
        core.reshape(1), tokens, other_tokens, key_grad, other_key_grad, cos, sin
    )
    both, partial = pair(xh.reshape(1), shard, across, partial)
    blocks = gather(both)
    near = lax.all_to_all(partial.reshape(16, 256, kvw // 2), NEAR, 0, 0)
    near_sum = near_total(near.reshape(8, 2, 256, kvw // 2), blocks[3], blocks[7])
    far = lax.all_to_all(near_sum, FAR, 0, 0, tiled=True)
    summed = far.reshape(64, 4, kvw).astype(jnp.float32).sum(0)
    count = rows * math.prod(SIZES.values())

    where = jnp.stack([core, lax.axis_index(("yh", "yl"))])
    p_own, t_own, p_sent, t_sent = forward(
        where, tokens, other_tokens, key_grad, other_key_grad, cos, sin, blocks, near_sum
    )
    p_other = lax.ppermute(p_sent, "c", SWAP)
    t_other = lax.ppermute(t_sent, "c", SWAP)
    rotated, token_grad = finish(core.reshape(1), p_own, t_own, p_other, t_other, cos, sin)
    weight_grad = (summed * (1.0 / math.sqrt(count))).astype(jnp.bfloat16)
    return (rotated, token_grad, weight_grad)


def solution(mesh):
    fine = Mesh(mesh.devices.reshape(tuple(SIZES.values())), tuple(SIZES))
    everywhere = P(REP + FSDP, None)
    return jax.shard_map(
        body,
        mesh=fine,
        in_specs=(everywhere, P(FSDP, None), P(FSDP), everywhere),
        out_specs=(everywhere, everywhere, everywhere),
        check_vma=False,
    )
```

```python
import math

import jax
import jax.numpy as jnp
from jax import lax
from jax.experimental import pallas as pl
from jax.experimental.pallas import tpu as pltpu
from jax.sharding import Mesh
from jax.sharding import PartitionSpec as P

HEAD_DIM = 128
HALF = HEAD_DIM // 2
rope_base = 10000.0

SIZES = {"xl": 2, "zh": 8, "zl": 2, "xh": 2, "yh": 4, "yl": 2, "c": 2}
REP = ("xl", "zh", "zl")
FSDP = ("xh", "yh", "yl", "c")
NEAR = ("xl", "zl", "xh", "c")
FAR = ("zh", "yh", "yl")
SWAP = [(0, 1), (1, 0)]
GRANT = 8 * 2**20
WIDE = 56 * 2**20
QUICK = pl.CostEstimate(flops=0, bytes_accessed=0, transcendentals=0)


def dequantize_kernel(scales, quant, out):
    rows, groups = quant.shape[0], scales.shape[1]
    group = lax.broadcasted_iota(jnp.int32, (rows, groups), 0) // (rows // groups)
    lane = lax.broadcasted_iota(jnp.int32, (rows, groups), 1)
    spread = jnp.where(group == lane, scales[...].astype(jnp.float32), 0.0)
    scale = jnp.sum(spread, axis=1, keepdims=True)
    out[...] = (quant[...].astype(jnp.float32) * scale).astype(jnp.bfloat16)


def dequantize(quant_weight, block_scales):
    return pl.pallas_call(
        dequantize_kernel,
        out_shape=jax.ShapeDtypeStruct(quant_weight.shape, jnp.bfloat16),
        compiler_params=pltpu.CompilerParams(vmem_limit_bytes=GRANT),
        cost_estimate=QUICK,
        name="dequantize",
    )(block_scales.reshape(1, -1), quant_weight)


def pair_kernel(here, own, across, passed, out, passed_on):
    out[here[0]] = own[...]
    out[1 - here[0]] = across[...]


def pair(here, own, across, passed):
    vmem = pl.BlockSpec(memory_space=pltpu.VMEM)
    anywhere = pl.BlockSpec(memory_space=pl.ANY)
    return pl.pallas_call(
        pair_kernel,
        out_shape=(
            jax.ShapeDtypeStruct((2,) + own.shape, own.dtype),
            jax.ShapeDtypeStruct(passed.shape, passed.dtype),
        ),
        in_specs=[pl.BlockSpec(memory_space=pltpu.SMEM), vmem, vmem, anywhere],
        out_specs=(vmem, anywhere),
        input_output_aliases={3: 1},
        compiler_params=pltpu.CompilerParams(vmem_limit_bytes=GRANT),
        cost_estimate=QUICK,
        name="pair",
    )(here, own, across, passed)


def gather(across_xh):
    right = [(i, (i + 1) % 8) for i in range(8)]
    left = [(i, (i + 7) % 8) for i in range(8)]
    axes = ("yh", "yl")
    rights, lefts = [across_xh], [across_xh]
    for _ in range(3):
        rights.append(lax.ppermute(rights[-1], axes, right))
        lefts.append(lax.ppermute(lefts[-1], axes, left))
    rights.append(lax.ppermute(rights[-1], axes, right))
    return rights + lefts[1:]


def near_kernel(near, after_right, after_left, out):
    chips, cores, rows, width = near.shape
    for r in range(0, rows, 16):
        at = slice(r, r + 16)
        for c in range(cores):
            total = near[0, c, at].astype(jnp.float32)
            for chip in range(1, chips):
                total = total + near[chip, c, at].astype(jnp.float32)
            out[at, c * width : (c + 1) * width] = total.astype(jnp.bfloat16)


def near_total(near, after_right, after_left):
    chips, cores, rows, width = near.shape
    vmem = pl.BlockSpec(memory_space=pltpu.VMEM)
    anywhere = pl.BlockSpec(memory_space=pl.ANY)
    return pl.pallas_call(
        near_kernel,
        out_shape=jax.ShapeDtypeStruct((rows, cores * width), jnp.bfloat16),
        in_specs=[vmem, anywhere, anywhere],
        out_specs=vmem,
        compiler_params=pltpu.CompilerParams(vmem_limit_bytes=GRANT),
        cost_estimate=QUICK,
        name="near_total",
    )(near, after_right, after_left)


def tables(positions):
    lane = jnp.arange(HEAD_DIM, dtype=jnp.int32)
    steps = (lane % HALF).astype(jnp.float32)
    frequency = jnp.exp(steps * (-2.0 * math.log(rope_base) / HEAD_DIM))
    angles = positions.astype(jnp.float32)[:, None] * frequency[None, :]
    sign = jnp.where(lane < HALF, -1.0, 1.0)[None, :]
    return jnp.cos(angles), sign * jnp.sin(angles)


def turn(values, cosine, sine, heads):
    parts = []
    for h in range(heads):
        part = values[:, h * HEAD_DIM : (h + 1) * HEAD_DIM]
        parts.append(part * cosine + pltpu.roll(part, HALF, 1) * sine)
    return parts


def grad_kernel(core, own, other, kg_own, kg_other, cos, sin, out, proj_grad):
    rows, features = own.shape
    width = proj_grad.shape[1]
    mine = pl.multiple_of(core[0] * width, width)
    for k, source in enumerate((kg_own, kg_other)):
        at = pl.ds(k * rows, rows)
        values = source[:, pl.ds(mine, width)].astype(jnp.float32)
        parts = turn(values, cos[at, :], -sin[at, :], width // HEAD_DIM)
        for h, part in enumerate(parts):
            proj_grad[at, h * HEAD_DIM : (h + 1) * HEAD_DIM] = part.astype(jnp.bfloat16)

    low = lax.broadcasted_iota(jnp.int32, (8, width), 0) < 4
    for block in range(features // 256):
        at = slice(block * 256, (block + 1) * 256)
        partial = lax.dot_general(
            jnp.concatenate([own[:, at], other[:, at]], 0),
            proj_grad[...],
            (((0,), (0,)), ((), ())),
            preferred_element_type=jnp.float32,
        )
        xl, zh = divmod(block, 8)
        for k in range(4):
            first, second = [], []
            for y in range(0, 8, 2):
                start = k * 64 + y * 8
                even, odd = partial[start : start + 8], partial[start + 8 : start + 16]
                first.append(jnp.where(low, even, pltpu.roll(odd, 4, 0)))
                second.append(jnp.where(low, pltpu.roll(even, 4, 0), odd))
            out[xl, k, 0, zh] = jnp.concatenate(first, 0).astype(jnp.bfloat16)
            out[xl, k, 1, zh] = jnp.concatenate(second, 0).astype(jnp.bfloat16)


def weight_partial(core, own, other, kg_own, kg_other, cos, sin):
    rows, features = own.shape
    kvw = kg_own.shape[1]
    vmem = pl.BlockSpec(memory_space=pltpu.VMEM)
    return pl.pallas_call(
        grad_kernel,
        out_shape=jax.ShapeDtypeStruct((2, 4, 2, 8, 32, kvw // 2), jnp.bfloat16),
        in_specs=[pl.BlockSpec(memory_space=pltpu.SMEM)] + [vmem] * 6,
        out_specs=vmem,
        scratch_shapes=[pltpu.VMEM((2 * rows, kvw // 2), jnp.bfloat16)],
        compiler_params=pltpu.CompilerParams(vmem_limit_bytes=GRANT),
        cost_estimate=pl.CostEstimate(
            flops=2 * rows * features * kvw, bytes_accessed=8 * 2**20, transcendentals=0
        ),
        name="weight_partial",
    )(core, own, other, kg_own, kg_other, cos, sin)


def forward_kernel(core_ref, y_ref, own, other, kg_own, kg_other, cos, sin, *refs):
    blocks, (after, p_out, t_out, p_sent, t_sent) = refs[:8], refs[8:13]
    t_own, t_other, held, kg, weights, proj_grad, total, sems = refs[13:]
    rows, kvw = kg_own.shape
    core, y = core_ref[0], y_ref[0]
    part = rows // 4
    pairs = [(kg_own, kg.at[pl.ds(0, rows)]), (kg_other, kg.at[pl.ds(rows, rows)])]
    pairs += [(block, weights.at[k]) for k, block in enumerate(blocks)]
    pairs += [
        (source.at[pl.ds(q * part, part)], held.at[pl.ds(k * rows + q * part, part)])
        for k, source in enumerate((own, other))
        for q in range(4)
    ]
    loads = [pltpu.make_async_copy(a, b, sems.at[i]) for i, (a, b) in enumerate(pairs)]
    for copy in loads:
        copy.start()
    for k in range(2):
        at = pl.ds(k * rows, rows)
        loads[k].wait()
        parts = turn(kg[at, :].astype(jnp.float32), cos[at, :], -sin[at, :], kvw // HEAD_DIM)
        for h, p in enumerate(parts):
            proj_grad[at, h * HEAD_DIM : (h + 1) * HEAD_DIM] = p.astype(jnp.bfloat16)

    def column(k, xh):
        return xh * 8 + lax.rem(y + (8 - k if k <= 4 else k - 4), 8)

    for k in range(8):
        loads[2 + k].wait()
        back = lax.dot_general(
            proj_grad[...],
            weights[k].reshape(256, kvw),
            (((1,), (1,)), ((), ())),
            preferred_element_type=jnp.float32,
        ).astype(jnp.bfloat16)
        for xh in range(2):
            at = pl.ds(pl.multiple_of(column(k, xh) * 128, 128), 128)
            half = slice(xh * 128, (xh + 1) * 128)
            t_own[:, at] = back[:rows, half]
            t_other[:, at] = back[rows:, half]
    stores = [
        pltpu.make_async_copy(t_other, t_sent, sems.at[0]),
        pltpu.make_async_copy(t_own, t_out, sems.at[1]),
        pltpu.make_async_copy(total.at[pl.ds(rows, rows)], p_sent, sems.at[2]),
        pltpu.make_async_copy(total.at[pl.ds(0, rows)], p_out, sems.at[3]),
    ]
    for store in stores[:2]:
        store.start()
    for copy in loads[10:]:
        copy.wait()
    for k in range(8):
        taken = [
            held[:, pl.ds(pl.multiple_of(column(k, xh) * 256 + core * 128, 128), 128)]
            for xh in range(2)
        ]
        share = jnp.dot(
            jnp.concatenate(taken, 1),
            weights[k].reshape(256, kvw),
            preferred_element_type=jnp.float32,
        )
        total[...] = share if k == 0 else total[...] + share
    for store in stores[2:]:
        store.start()
    for copy in stores:
        copy.wait()


def forward(core, y, own, other, kg_own, kg_other, cos, sin, blocks, after):
    rows, features = own.shape
    kvw = kg_own.shape[1]
    vmem = pl.BlockSpec(memory_space=pltpu.VMEM)
    anywhere = pl.BlockSpec(memory_space=pl.ANY)
    return pl.pallas_call(
        forward_kernel,
        out_shape=(
            jax.ShapeDtypeStruct((rows, kvw), jnp.float32),
            jax.ShapeDtypeStruct((rows, features // 2), jnp.bfloat16),
            jax.ShapeDtypeStruct((rows, kvw), jnp.float32),
            jax.ShapeDtypeStruct((rows, features // 2), jnp.bfloat16),
        ),
        in_specs=[pl.BlockSpec(memory_space=pltpu.SMEM)] * 2
        + [anywhere] * 4
        + [vmem] * 2
        + [anywhere] * 9,
        out_specs=[anywhere] * 4,
        scratch_shapes=[
            pltpu.VMEM((rows, features // 2), jnp.bfloat16),
            pltpu.VMEM((rows, features // 2), jnp.bfloat16),
            pltpu.VMEM((2 * rows, features), jnp.bfloat16),
            pltpu.VMEM((2 * rows, kvw), jnp.bfloat16),
            pltpu.VMEM((8,) + blocks[0].shape, jnp.bfloat16),
            pltpu.VMEM((2 * rows, kvw), jnp.bfloat16),
            pltpu.VMEM((2 * rows, kvw), jnp.float32),
            pltpu.SemaphoreType.DMA((18,)),
        ],
        compiler_params=pltpu.CompilerParams(vmem_limit_bytes=WIDE),
        cost_estimate=QUICK,
        name="forward",
    )(core, y, own, other, kg_own, kg_other, cos, sin, *blocks, after)


def finish_kernel(core, p_own, t_own, p_other, t_other, cos, sin, rotated, token_grad):
    kvw = p_own.shape[1]
    total = p_own[...] + p_other[...]
    for h, part in enumerate(turn(total, cos[...], sin[...], kvw // HEAD_DIM)):
        rotated[:, h * HEAD_DIM : (h + 1) * HEAD_DIM] = part.astype(jnp.bfloat16)
    for f in range(t_own.shape[1] // 128):
        at = slice(f * 128, (f + 1) * 128)
        for source, parity in ((t_own, core[0]), (t_other, 1 - core[0])):
            column = pl.multiple_of(f * 256 + parity * 128, 128)
            token_grad[:, pl.ds(column, 128)] = source[:, at]


def finish(core, p_own, t_own, p_other, t_other, cos, sin):
    rows, kvw = p_own.shape
    features = 2 * t_own.shape[1]
    steps = 3
    block = lambda width: pl.BlockSpec((rows // steps, width), lambda s: (s, 0))
    return pl.pallas_call(
        finish_kernel,
        grid=(steps,),
        out_shape=(
            jax.ShapeDtypeStruct((rows, kvw), jnp.bfloat16),
            jax.ShapeDtypeStruct((rows, features), jnp.bfloat16),
        ),
        in_specs=[pl.BlockSpec(memory_space=pltpu.SMEM)]
        + [block(kvw), block(features // 2)] * 2
        + [block(HEAD_DIM)] * 2,
        out_specs=(block(kvw), block(features)),
        compiler_params=pltpu.CompilerParams(vmem_limit_bytes=GRANT),
        cost_estimate=QUICK,
        name="finish",
    )(core, p_own, t_own, p_other, t_other, cos, sin)


def body(tokens, quant_weight, block_scales, key_grad):
    rows = tokens.shape[0]
    kvw = key_grad.shape[1]
    core = lax.axis_index("c")
    xh = lax.axis_index("xh")
    place = lax.axis_index(FSDP)

    shard = dequantize(quant_weight, block_scales)
    across = lax.ppermute(shard, ("xl", "xh"), [(i, 3 - i) for i in range(4)])
    other_tokens = lax.ppermute(tokens, "c", SWAP)
    other_key_grad = lax.ppermute(key_grad, "c", SWAP)

    offsets = jnp.arange(rows, dtype=jnp.int32)
    positions = jnp.concatenate([place * rows + offsets, (place + 1 - 2 * core) * rows + offsets])
    cos, sin = tables(positions)

    partial = weight_partial(
        core.reshape(1), tokens, other_tokens, key_grad, other_key_grad, cos, sin
    )
    both, partial = pair(xh.reshape(1), shard, across, partial)
    blocks = gather(both)
    near = lax.all_to_all(partial.reshape(16, 256, kvw // 2), NEAR, 0, 0)
    near_sum = near_total(near.reshape(8, 2, 256, kvw // 2), blocks[3], blocks[7])
    far = lax.all_to_all(near_sum, FAR, 0, 0, tiled=True)
    p_own, t_own, p_sent, t_sent = forward(
        core.reshape(1),
        lax.axis_index(("yh", "yl")).reshape(1),
        tokens,
        other_tokens,
        key_grad, other_key_grad, cos, sin, blocks, near_sum
    )
    p_other = lax.ppermute(p_sent, "c", SWAP)
    t_other = lax.ppermute(t_sent, "c", SWAP)
    rotated, token_grad = finish(core.reshape(1), p_own, t_own, p_other, t_other, cos, sin)
    count = rows * math.prod(SIZES.values())
    scaled = far.reshape(64, 4, kvw).astype(jnp.float32) * (1.0 / math.sqrt(count))
    weight_grad = scaled.sum(0).astype(jnp.bfloat16)
    return (rotated, token_grad, weight_grad)


def solution(mesh):
    fine = Mesh(mesh.devices.reshape(tuple(SIZES.values())), tuple(SIZES))
    everywhere = P(REP + FSDP, None)
    return jax.shard_map(
        body,
        mesh=fine,
        in_specs=(everywhere, P(FSDP, None), P(FSDP), everywhere),
        out_specs=(everywhere, everywhere, everywhere),
        check_vma=False,
    )
```
